256 devices in a mesh: seq: 16 (over z_hi, x, core), chan: 16 (over y, z_lo).
Axes of the slice: x: 4, y: 4, z: 8 (z_hi: 2, z_lo: 4; z = z_hi * 4 + z_lo), core: 2. Of those that a mesh axis runs over, the one named last changes fastest.
Arguments:
- layer_input: bfloat16 [65536, 2560], P('seq', 'chan'), may hold values from -6 to 6
- query_scale: float32 [2560], P('chan'), may hold values from 0.5 to 2
- key_scale: float32 [2560], P('chan'), may hold values from 0.5 to 2
- twiddle: float32 [128, 512], P('seq'), may hold values from 0.5 to 2
- seq_inner: bfloat16 [512, 512], replicated, may hold values from -0.25 to 0.25
- seq_outer: bfloat16 [128, 128], replicated, may hold values from -0.5 to 0.5
- grad_output: bfloat16 [65536, 2560], P('seq', 'chan'), may hold values from -6 to 6
- hidden_pre: bfloat16 [65536, 6144], P('seq', 'chan'), may hold values from -8 to 8
- up_right: bfloat16 [16, 384, 640], P('chan'), may hold values from -0.25 to 0.25
- up_left: bfloat16 [4, 4, 1536], replicated, may hold values from -3 to 3
- down_right: bfloat16 [16, 640, 384], P('chan'), may hold values from -0.15625 to 0.15625
- down_left: bfloat16 [4, 4, 640], replicated, may hold values from -3 to 3
Outputs:
- grad_input: bfloat16 [65536, 2560], P('seq', 'chan')
- grad_up_right: float32 [16, 384, 640], P('chan', None, 'seq')
- grad_down_right: float32 [16, 640, 384], P('chan', 'seq')
- grad_query_scale: float32 [2560], P('chan')
- grad_key_scale: float32 [2560], P('chan')
- grad_seq_inner: float32 [512, 512], replicated
- grad_seq_outer: float32 [128, 128], replicated
The draws below stay inside these ranges and needn't reach their ends.
All inputs are finite; a program needn't handle non-finite values.
Results may differ from the reference program's by a relative error of at most 0.0077.
Values may be sent and summed in bfloat16 or wider, within the bound.
No kernel may reach another device: no remote copies, remote signals or barrier semaphores. Data moves between devices by JAX's collectives and lax.ppermute only.
A program may use at most 128 MiB of HBM per device.

```python
import math
import jax
import jax.numpy as jnp
from jax import lax

D = 2560
NB = 4
HID = 6144
A = 128
B = 512
G = 640
HB = 1536
L = 65536
GS = 4
QS = 384
N_CHAN = 16


def block_levels(rng, dims, shards, least, top_value):
    gain = 1.0
    for axis_at, blocks in shards:
        steps = jax.random.uniform(jax.random.fold_in(jax.random.fold_in(rng, 6), axis_at), (blocks,), jnp.float32, least / len(shards), top_value / len(shards))
        gain = gain * jnp.repeat(jnp.exp(steps), dims[axis_at] // blocks).reshape((-1,) + (1,) * (len(dims) - 1 - axis_at))
    return gain


def normal_values(stream_key, dims, deviation, reach, pieces=(), kind=jnp.bfloat16):
    entries = deviation * jax.random.normal(stream_key, dims, jnp.float32)
    if pieces:
        entries = entries * block_levels(stream_key, dims, pieces, -0.22, 0.18)
    return jnp.clip(entries, -reach, reach).astype(kind)


def setup_inputs(seed: int = 0) -> dict:
    seeds = jax.random.split(jax.random.key(seed), 13)
    return {
        "layer_input": normal_values(seeds[0], (L, D), 1.0, 6.0, ((0, 16), (1, 16))),
        "query_scale": jnp.clip(jnp.exp(math.log(2.0) - 1.3862944 * jax.random.uniform(seeds[1], (D,), jnp.float32) ** block_levels(seeds[1], (D,), ((0, 16),), -0.2, 0.2)), 0.5, 2.0),
        "key_scale": jnp.clip(jnp.exp(math.log(2.0) - 1.3862944 * jax.random.uniform(seeds[2], (D,), jnp.float32) ** block_levels(seeds[2], (D,), ((0, 16),), -0.2, 0.2)), 0.5, 2.0),
        "twiddle": jnp.clip(jnp.exp(math.log(2.0) - 1.3862944 * jax.random.uniform(seeds[3], (A, B), jnp.float32) ** block_levels(seeds[3], (A, B), ((0, 16),), -0.2, 0.2)), 0.5, 2.0),
        "seq_inner": normal_values(seeds[4], (B, B), B ** -0.5, 0.25),
        "seq_outer": normal_values(seeds[5], (A, A), A ** -0.5, 0.5),
        "grad_output": normal_values(seeds[6], (L, D), 1.0, 6.0, ((0, 16), (1, 16))),
        "hidden_pre": normal_values(seeds[7], (L, HID), 1.5, 8.0, ((0, 16), (1, 16))),
        "up_right": normal_values(seeds[8], (NB * GS, QS, G), G ** -0.5, 0.25, ((0, 16),)),
        "up_left": normal_values(seeds[9], (NB, NB, HB), NB ** -0.5, 3.0),
        "down_right": normal_values(seeds[10], (NB * GS, G, QS), HB ** -0.5, 0.15625, ((0, 16),)),
        "down_left": normal_values(seeds[11], (NB, NB, G), NB ** -0.5, 3.0),
    }


def lower_mask(size):
    return jnp.arange(size)[:, None] >= jnp.arange(size)[None, :]

def round_trip(value):
    return lax.optimization_barrier(value.astype(jnp.bfloat16)).astype(jnp.float32)

def reference(layer_input, query_scale, key_scale, twiddle, seq_inner, seq_outer, grad_output, hidden_pre, up_right, up_left, down_right, down_left):
    group_size = N_CHAN // NB
    inner_tri = jnp.where(lower_mask(B), seq_inner, jnp.zeros_like(seq_inner)).astype(jnp.float32)
    outer_tri = jnp.where(lower_mask(A), seq_outer, jnp.zeros_like(seq_outer)).astype(jnp.float32)
    twiddle_f = twiddle.astype(jnp.float32)

    def forward_mix(block_input, query_part, key_part):
        inputs = block_input.astype(jnp.float32)
        key_input = (inputs * key_part).astype(jnp.bfloat16)
        first_pass = (jnp.einsum('bk,akc->abc', inner_tri, key_input.astype(jnp.float32)) * twiddle_f[:, :, None]).astype(jnp.bfloat16)
        convolved = jnp.einsum('ij,jbc->ibc', outer_tri, first_pass.astype(jnp.float32)).astype(jnp.bfloat16)
        return (key_input, first_pass, convolved)
    split_input = layer_input.reshape(A, B, NB, G).transpose(2, 0, 1, 3)
    query_blocks = query_scale.reshape(NB, G)
    key_blocks = key_scale.reshape(NB, G)

    def mix_block(slices):
        block_input, query_part, key_part = slices
        key_input, first_pass, convolved = forward_mix(block_input, query_part, key_part)
        inputs = block_input.astype(jnp.float32)
        return (inputs + inputs * query_part * convolved.astype(jnp.float32)).astype(jnp.bfloat16)
    mixed = lax.map(mix_block, (split_input, query_blocks, key_blocks))
    mixed_rows = mixed.transpose(1, 2, 0, 3).reshape(A, B, D)
    right_up = up_right.reshape(NB, group_size, HB // group_size, G).astype(jnp.float32)
    right_down = down_right.reshape(NB, group_size, G, HB // group_size).transpose(0, 2, 1, 3).reshape(NB, G, HB).astype(jnp.float32)
    left_up = up_left.astype(jnp.float32)
    left_down = down_left.astype(jnp.float32)

    def mlp_rows(totals, slices):
        up_total, down_total = totals
        mix_rows, out_rows, pre_rows = slices
        mix_blocks = mix_rows.reshape(B, NB, G).astype(jnp.float32)
        out_blocks = out_rows.reshape(B, NB, G).astype(jnp.float32)
        down_grad = round_trip(jnp.einsum('jkp,tjp->tkp', left_down, out_blocks))
        hidden_grad = jnp.einsum('kpq,tkp->tkq', right_down, down_grad)
        pre_values = pre_rows.reshape(B, NB, HB).astype(jnp.float32)
        activated = round_trip(jax.nn.gelu(pre_values))
        down_total = down_total + jnp.einsum('tkp,tkq->kpq', down_grad, activated)
        pre_grad = round_trip(jax.vjp(jax.nn.gelu, pre_values)[1](hidden_grad)[0])
        right_grad = round_trip(jnp.einsum('jkq,tjq->tkq', left_up, pre_grad))
        up_total = up_total + jnp.einsum('tkq,tkp->kqp', right_grad, mix_blocks)
        parts = jnp.einsum('ksqp,tksq->tksp', right_up, right_grad.reshape(B, NB, group_size, HB // group_size))
        mix_grad = out_blocks + lax.optimization_barrier(jnp.sum(round_trip(parts), axis=2))
        return ((up_total, down_total), mix_grad.reshape(B, D))
    start = (jnp.zeros((NB, HB, G), jnp.float32), jnp.zeros((NB, G, HB), jnp.float32))
    (up_total, down_total), mix_grad = lax.scan(mlp_rows, start, (mixed_rows, grad_output.reshape(A, B, D), hidden_pre.reshape(A, B, HID)))
    token_scale = (A * B) ** (-0.5)
    grad_up_right = (up_total * token_scale).reshape(NB * group_size, HB // group_size, G)
    grad_down_right = (down_total * token_scale).reshape(NB, G, group_size, HB // group_size).transpose(0, 2, 1, 3).reshape(NB * group_size, G, HB // group_size)
    grad_blocks = mix_grad.reshape(A, B, NB, G).transpose(2, 0, 1, 3)

    def back_block(totals, slices):
        inner_total, outer_total = totals
        block_input, query_part, key_part, block_grad = slices
        key_input, first_pass, convolved = forward_mix(block_input, query_part, key_part)
        inputs = block_input.astype(jnp.float32)
        conv_f = convolved.astype(jnp.float32)
        conv_grad = round_trip(block_grad * inputs * query_part)
        query_total = lax.optimization_barrier(jnp.sum(block_grad * inputs * conv_f, axis=(0, 1)))
        first_grad = round_trip(jnp.einsum('ij,ibc->jbc', outer_tri, conv_grad))
        outer_total = outer_total + jnp.einsum('ibc,jbc->ij', conv_grad, first_pass.astype(jnp.float32))
        back_pass = round_trip(first_grad * twiddle_f[:, :, None])
        key_grad = jnp.einsum('bk,abc->akc', inner_tri, back_pass)
        inner_total = inner_total + jnp.einsum('abc,akc->bk', back_pass, key_input.astype(jnp.float32))
        input_grad = (block_grad * (1.0 + query_part * conv_f) + key_part * key_grad).astype(jnp.bfloat16)
        key_total = lax.optimization_barrier(jnp.sum(key_grad * inputs, axis=(0, 1)))
        return ((inner_total, outer_total), (input_grad, query_total, key_total))
    start = (jnp.zeros((B, B), jnp.float32), jnp.zeros((A, A), jnp.float32))
    (inner_total, outer_total), (input_grad, query_total, key_total) = lax.scan(back_block, start, (split_input, query_blocks, key_blocks, grad_blocks))
    grad_input = input_grad.transpose(1, 2, 0, 3).reshape(A * B, D)
    grad_query_scale = query_total.reshape(D) * token_scale
    grad_key_scale = key_total.reshape(D) * token_scale
    grad_seq_inner = jnp.where(lower_mask(B), inner_total, jnp.zeros_like(inner_total)) * (A * D) ** (-0.5)
    grad_seq_outer = jnp.where(lower_mask(A), outer_total, jnp.zeros_like(outer_total)) * (B * D) ** (-0.5)
    return (grad_input, grad_up_right, grad_down_right, grad_query_scale, grad_key_scale, grad_seq_inner, grad_seq_outer)
```

```python
import jax
import jax.numpy as jnp
from jax import lax
from jax.sharding import PartitionSpec as P

BF = jnp.bfloat16
F32 = jnp.float32
BLOCKS = 4
GROUP = 4
SEQ = 16
CHAN = 16
Z_LO = [0, 1, 2, 3]
Y = [0, 4, 8, 12]
CORE = [0, 16]
X = [0, 32, 64, 96]
Z_HI = [0, 128]


def join(high, low):
    return [h ^ l for h in high for l in low]


def swap(value, mask):
    if mask == 0:
        return value
    route = [(i, i ^ mask) for i in range(SEQ * CHAN)]
    return lax.ppermute(value, ("seq", "chan"), route)


def spread(take, me, masks, out_shape, dtype, axis):
    size = out_shape[axis] // len(masks)
    out = jnp.zeros(out_shape, dtype)
    for step, mask in enumerate(masks):
        other = jnp.bitwise_xor(me, step)
        arrived = swap(take(other), mask)
        out = lax.dynamic_update_slice_in_dim(out, arrived, other * size, axis)
    return out


def part_of(value, index, count, axis):
    size = value.shape[axis] // count
    return lax.dynamic_slice_in_dim(value, index * size, size, axis)


def sum_spread(take, me, masks):
    total = None
    for step, mask in enumerate(masks):
        piece = take(jnp.bitwise_xor(me, step))
        arrived = swap(piece.astype(BF), mask).astype(F32) if mask else piece.astype(F32)
        total = arrived if total is None else total + arrived
    return total


def sum_spread_f32(take, me, masks):
    total = None
    for step, mask in enumerate(masks):
        arrived = swap(take(jnp.bitwise_xor(me, step)), mask)
        total = arrived if total is None else total + arrived
    return total


def gather(value, me, masks, axis):
    shape = list(value.shape)
    shape[axis] *= len(masks)
    return spread(lambda other: value, me, masks, tuple(shape), value.dtype, axis)


def seq_exchange(value, core, zx):
    rows, width = value.shape[1:]
    by_core = value.reshape(8, 2, rows, width)
    near = spread(
        lambda other: lax.dynamic_index_in_dim(by_core, other, 1, keepdims=True).transpose(1, 0, 2, 3),
        core, CORE, (2, 8, rows, width), value.dtype, 0,
    )
    near = near.transpose(1, 0, 2, 3)
    far = spread(
        lambda other: lax.dynamic_index_in_dim(near, other, 0, keepdims=True),
        zx, join(Z_HI, X), (8, 2, rows, width), value.dtype, 0,
    )
    return far.reshape(16, rows, width)


def lower_mask(size):
    return jnp.arange(size)[:, None] >= jnp.arange(size)[None, :]


def weight_total(terms, core, x, z_hi, z_lo):
    split = terms.reshape(8, 2, terms.shape[0] // 16, terms.shape[1])
    pair = sum_spread(lambda other: lax.dynamic_index_in_dim(split, other, 1, keepdims=False), core, CORE)
    pair = pair.reshape((2, 4) + pair.shape[1:])
    line = sum_spread(lambda other: lax.dynamic_index_in_dim(pair, other, 1, keepdims=False), x, X)

    def take(other):
        rows = lax.dynamic_index_in_dim(line, other // 4, 0, keepdims=False)
        return part_of(rows, other % 4, 4, 1)

    return sum_spread(take, z_hi * 4 + z_lo, join(Z_HI, Z_LO))


def body(
    layer_input,
    query_scale,
    key_scale,
    twiddle,
    seq_inner,
    seq_outer,
    grad_output,
    hidden_pre,
    up_right,
    up_left,
    down_right,
    down_left,
):
    outer_here, inner_len = twiddle.shape
    tokens, width = layer_input.shape
    outer_len = seq_outer.shape[0]
    hidden = hidden_pre.shape[1]
    quarter = tokens // GROUP
    seq = lax.axis_index("seq")
    chan = lax.axis_index("chan")
    z_lo, y = chan % 4, chan // 4
    core, x, z_hi = seq % 2, (seq // 2) % 4, seq // 8
    zx = seq // 2
    mine = width // SEQ
    inner_mask = lower_mask(inner_len)
    outer_mask = lower_mask(outer_len)
    inner_tri = jnp.where(inner_mask, seq_inner, jnp.zeros_like(seq_inner))
    outer_tri = jnp.where(outer_mask, seq_outer, jnp.zeros_like(seq_outer))
    layer_t = layer_input.T
    grad_t = grad_output.T

    pre_values = spread(
        lambda other: part_of(hidden_pre, other, 4, 0), z_lo, Z_LO, (quarter, 4 * hidden), BF, 1
    )

    grad_split = grad_t.reshape(width, GROUP, BLOCKS, quarter // BLOCKS)
    grad_blocks = spread(
        lambda other: lax.dynamic_index_in_dim(grad_split, other, 2, keepdims=False)[None],
        y, Y, (BLOCKS, width, GROUP, quarter // BLOCKS), BF, 0,
    )
    left_here = part_of(down_left, z_lo, 4, 2).astype(F32)
    grad_blocks = grad_blocks.astype(F32)
    down_mix = jnp.stack(
        [
            sum(left_here[j, k][:, None, None] * grad_blocks[j] for j in range(BLOCKS)).astype(BF)
            for k in range(BLOCKS)
        ]
    )
    down_here = spread(
        lambda other: lax.dynamic_index_in_dim(down_mix, other, 0, keepdims=False)[:, :, None],
        y, Y, (width, GROUP, BLOCKS, quarter // BLOCKS), BF, 2,
    ).reshape(width, tokens)
    down_grad = spread(
        lambda other: part_of(down_here, other, 4, 1), z_lo, Z_LO, (4 * width, quarter), BF, 0
    )

    right = jnp.stack([down_right[0], up_right[0].T])
    right = part_of(right, seq % 8, 8, 1)
    right = gather(right, z_lo, Z_LO, 2)
    right = gather(right, core, CORE, 1)
    right = gather(right, x, X, 1)

    layer_rows = layer_t.reshape(SEQ, mine * outer_here, inner_len)
    layer_cols = seq_exchange(layer_rows, core, zx)

    def to_cols(value):
        return (
            value.reshape(SEQ, mine, outer_here, inner_len)
            .transpose(1, 0, 2, 3)
            .reshape(mine, outer_len, inner_len)
        )

    def to_rows(value):
        return (
            value.reshape(mine, SEQ, outer_here, inner_len)
            .transpose(1, 0, 2, 3)
            .reshape(SEQ, mine * outer_here, inner_len)
        )

    twiddle_all = gather(gather(twiddle, core, CORE, 0), zx, join(Z_HI, X), 0)
    layer_cols = to_cols(layer_cols).astype(F32)
    key_mine = part_of(key_scale, seq, SEQ, 0)[:, None, None]
    query_mine = part_of(query_scale, seq, SEQ, 0)
    key_input = (layer_cols * key_mine).astype(BF)
    first_pass = (
        jnp.einsum("bk,cak->cab", inner_tri, key_input, preferred_element_type=F32) * twiddle_all
    ).astype(BF)
    conv_cols = jnp.einsum("ij,cjb->cib", outer_tri, first_pass, preferred_element_type=F32).astype(BF)
    convolved = seq_exchange(to_rows(conv_cols), core, zx).reshape(width, tokens).astype(F32)
    inputs = layer_t.astype(F32)
    query_col = query_scale[:, None]
    mixed = (inputs + inputs * query_col * convolved).astype(BF)
    mixed_rows = spread(
        lambda other: part_of(mixed, other, 4, 1), z_lo, Z_LO, (4 * width, quarter), BF, 0
    )

    hidden_grad = jnp.einsum("pt,pq->tq", down_grad, right[0], preferred_element_type=F32)
    pre_f = pre_values.astype(F32)
    activated = jax.nn.gelu(pre_f).astype(BF)
    pre_grad = jax.vjp(jax.nn.gelu, pre_f)[1](hidden_grad)[0].astype(BF)
    down_terms = jnp.einsum("pt,tq->pq", down_grad, activated, preferred_element_type=F32)
    pre_blocks = spread(
        lambda other: part_of(pre_grad, other, 4, 0)[None],
        y, Y, (BLOCKS, quarter // BLOCKS, 4 * hidden), BF, 0,
    ).astype(F32)
    left_up = up_left.astype(F32)
    right_mix = jnp.stack(
        [
            sum(left_up[j, k][None, :] * pre_blocks[j] for j in range(BLOCKS)).astype(BF)
            for k in range(BLOCKS)
        ]
    )
    right_grad = spread(
        lambda other: lax.dynamic_index_in_dim(right_mix, other, 0, keepdims=False),
        y, Y, (quarter, 4 * hidden), BF, 0,
    )
    partial_value = jnp.einsum("pq,tq->pt", right[1], right_grad, preferred_element_type=F32).astype(BF)
    arrived = spread(
        lambda other: part_of(partial_value, other, 4, 0), z_lo, Z_LO, (width, tokens), BF, 1
    )
    up_terms = jnp.einsum("pt,tq->pq", mixed_rows, right_grad, preferred_element_type=F32)

    mix_grad = grad_t.astype(F32) + arrived.astype(F32)
    conv_grad = (mix_grad * inputs * query_col).astype(BF)
    conv_grad = to_cols(seq_exchange(conv_grad.reshape(SEQ, mine * outer_here, inner_len), core, zx))
    query_terms = jnp.sum(conv_grad.astype(F32) * conv_cols.astype(F32), axis=(1, 2)) / query_mine
    first_grad = jnp.einsum("ij,cib->cjb", outer_tri, conv_grad, preferred_element_type=F32).astype(BF)
    outer_terms = jnp.einsum("cib,cjb->ij", conv_grad, first_pass, preferred_element_type=F32)
    back_pass = (first_grad.astype(F32) * twiddle_all).astype(BF)
    key_grad = jnp.einsum("bk,cab->cak", inner_tri, back_pass, preferred_element_type=F32)
    inner_terms = jnp.einsum("cab,cak->bk", back_pass, key_input, preferred_element_type=F32)
    key_terms = jnp.sum(key_grad * layer_cols, axis=(1, 2))
    key_back = seq_exchange(to_rows((key_grad * key_mine).astype(BF)), core, zx)
    key_back = key_back.reshape(width, tokens).astype(F32)
    grad_input = (mix_grad * (1.0 + query_col * convolved) + key_back).astype(BF).T

    side = 128
    count = inner_len // side
    tiles = [
        inner_terms[i * side : (i + 1) * side, j * side : (j + 1) * side]
        for i in range(count)
        for j in range(i + 1)
    ]
    model = CHAN * width
    at = chan * width + seq * mine
    scales = jnp.zeros((2, model), F32)
    scales = lax.dynamic_update_slice(scales, jnp.stack([query_terms, key_terms]), (0, at))
    scale_rows = 2 * model // side
    sums = jnp.concatenate(tiles + [outer_terms, scales.reshape(scale_rows, side)], axis=0)
    whole_rows = -(-sums.shape[0] // 512) * 512
    sums = jnp.pad(sums, ((0, whole_rows - sums.shape[0]), (0, 0)))
    for me, masks in ((y, Y), (z_lo, Z_LO), (x, X)):
        sums = sum_spread_f32(lambda other, sums=sums: part_of(sums, other, 4, 0), me, masks)
    sums = sum_spread_f32(lambda other: sums, z_hi * 2 + core, join(Z_HI, CORE))
    for me, masks in ((x, X), (z_lo, Z_LO), (y, Y)):
        sums = gather(sums, me, masks, 0)
    blank = jnp.zeros((side, side), F32)
    rows, taken = [], 0
    for i in range(count):
        rows.append(
            jnp.concatenate(
                [sums[(taken + j) * side : (taken + j + 1) * side] for j in range(i + 1)]
                + [blank] * (count - 1 - i),
                axis=1,
            )
        )
        taken += i + 1
    inner_total = jnp.where(inner_mask, jnp.concatenate(rows, axis=0), 0.0)
    outer_total = jnp.where(outer_mask, sums[taken * side : (taken + 1) * side], 0.0)
    scale_total = sums[(taken + 1) * side : (taken + 1) * side + scale_rows].reshape(2, model)
    scale_total = lax.dynamic_slice_in_dim(scale_total, chan * width, width, 1)

    token_scale = (SEQ * tokens) ** (-0.5)
    grad_down = weight_total(down_terms, core, x, z_hi, z_lo) * token_scale
    grad_up = weight_total(up_terms, core, x, z_hi, z_lo).T * token_scale
    return (
        grad_input,
        grad_up[None],
        grad_down[None],
        scale_total[0] * token_scale,
        scale_total[1] * token_scale,
        inner_total * (outer_len * model) ** (-0.5),
        outer_total * (inner_len * model) ** (-0.5),
    )


def solution(mesh):
    return jax.shard_map(
        body,
        mesh=mesh,
        in_specs=(
            P("seq", "chan"),
            P("chan"),
            P("chan"),
            P("seq", None),
            P(),
            P(),
            P("seq", "chan"),
            P("seq", "chan"),
            P("chan", None, None),
            P(),
            P("chan", None, None),
            P(),
        ),
        out_specs=(
            P("seq", "chan"),
            P("chan", None, "seq"),
            P("chan", "seq", None),
            P("chan"),
            P("chan"),
            P(),
            P(),
        ),
        check_vma=False,
    )
```

```python
import jax
import jax.numpy as jnp
from jax import lax
from jax.sharding import PartitionSpec as P

BF = jnp.bfloat16
F32 = jnp.float32
BLOCKS = 4
GROUP = 4
SEQ = 16
CHAN = 16
Z_LO = [0, 1, 2, 3]
Y = [0, 4, 8, 12]
CORE = [0, 16]
X = [0, 32, 64, 96]
Z_HI = [0, 128]


def join(high, low):
    return [h ^ l for h in high for l in low]


def swap(value, mask):
    if mask == 0:
        return value
    route = [(i, i ^ mask) for i in range(SEQ * CHAN)]
    return lax.ppermute(value, ("seq", "chan"), route)


def pieces_for(take, me, masks, behind=()):
    pieces = [take(jnp.bitwise_xor(me, step)) for step in range(len(masks))]
    return list(lax.optimization_barrier((*pieces, *behind))[: len(masks)])


def deliver(name, pieces, me, masks, axis, seen=None):
    size = pieces[0].shape[axis]
    shape = list(pieces[0].shape)
    shape[axis] = size * len(masks)
    out = jnp.zeros(shape, pieces[0].dtype)
    for step, mask in enumerate(masks):
        with jax.named_scope(name):
            arrived = swap(pieces[step], mask)
        if seen is not None:
            seen.append(arrived)
        out = lax.dynamic_update_slice_in_dim(out, arrived, jnp.bitwise_xor(me, step) * size, axis)
    return out


def after(value, *others):
    return lax.optimization_barrier((value, *others))[0]


def part_of(value, index, count, axis):
    size = value.shape[axis] // count
    return lax.dynamic_slice_in_dim(value, index * size, size, axis)


def sum_spread(name, take, me, masks):
    total = None
    for step, mask in enumerate(masks):
        piece = take(jnp.bitwise_xor(me, step))
        with jax.named_scope(name):
            arrived = swap(piece.astype(BF), mask).astype(F32) if mask else piece.astype(F32)
        total = arrived if total is None else total + arrived
    return total


def sum_spread_f32(name, take, me, masks):
    total = None
    for step, mask in enumerate(masks):
        with jax.named_scope(name):
            arrived = swap(take(jnp.bitwise_xor(me, step)), mask)
        total = arrived if total is None else total + arrived
    return total


def gather(name, value, me, masks, axis):
    return deliver(name, [value] * len(masks), me, masks, axis)


def seq_exchange(name, value):
    with jax.named_scope(name):
        return lax.all_to_all(value, "seq", split_axis=0, concat_axis=0, tiled=True)


def plane_exchange(name, value):
    groups = [list(range(8)), list(range(8, SEQ))]
    with jax.named_scope(name):
        return lax.all_to_all(
            value, "seq", split_axis=0, concat_axis=0, axis_index_groups=groups, tiled=True
        )


def group_exchange(name, value):
    groups = [list(range(first, first + GROUP)) for first in range(0, CHAN, GROUP)]
    with jax.named_scope(name):
        return lax.all_to_all(
            value, "chan", split_axis=0, concat_axis=0, axis_index_groups=groups, tiled=True
        )


def line_exchange(name, value):
    groups = [
        [(z_hi * 8 + plane) * CHAN + block * GROUP + z_lo for z_hi in range(2) for z_lo in range(GROUP)]
        for plane in range(8)
        for block in range(BLOCKS)
    ]
    with jax.named_scope(name):
        return lax.all_to_all(
            value, ("seq", "chan"), split_axis=0, concat_axis=0, axis_index_groups=groups, tiled=True
        )


def lower_mask(size):
    return jnp.arange(size)[:, None] >= jnp.arange(size)[None, :]


def weight_core(terms, core):
    count, rows, width = terms.shape
    split = terms.reshape(count, 8, 2, rows // 16, width)
    pair = sum_spread(
        "weight_core", lambda other: lax.dynamic_index_in_dim(split, other, 2, keepdims=False), core, CORE
    )
    return pair.reshape(count, 2, 4, rows // 16, width)


def weight_line(pair, x):
    return sum_spread(
        "weight_x", lambda other: lax.dynamic_index_in_dim(pair, other, 2, keepdims=False), x, X
    )


def weight_z(line, z_lo):
    return sum_spread("weight_z", lambda other: part_of(line, other, 4, 3), z_lo, Z_LO)


def weight_z_hi(line, z_hi):
    return sum_spread(
        "weight_z_hi", lambda other: lax.dynamic_index_in_dim(line, other, 1, keepdims=False), z_hi, Z_HI
    )


def body(
    layer_input,
    query_scale,
    key_scale,
    twiddle,
    seq_inner,
    seq_outer,
    grad_output,
    hidden_pre,
    up_right,
    up_left,
    down_right,
    down_left,
):
    outer_here, inner_len = twiddle.shape
    tokens, width = layer_input.shape
    outer_len = seq_outer.shape[0]
    hidden = hidden_pre.shape[1]
    quarter = tokens // GROUP
    seq = lax.axis_index("seq")
    chan = lax.axis_index("chan")
    z_lo, y = chan % 4, chan // 4
    core, x, z_hi = seq % 2, (seq // 2) % 4, seq // 8
    mine = width // SEQ
    inner_mask = lower_mask(inner_len)
    outer_mask = lower_mask(outer_len)
    inner_tri = jnp.where(inner_mask, seq_inner, jnp.zeros_like(seq_inner))
    outer_tri = jnp.where(outer_mask, seq_outer, jnp.zeros_like(seq_outer))
    layer_t = layer_input.T
    grad_t = grad_output.T
    piece = quarter // BLOCKS

    right = jnp.stack([down_right[0], up_right[0].T])
    right = part_of(right, core * 4 + x, 8, 1)

    grad_pieces = pieces_for(lambda other: part_of(grad_t, other, 4, 1), z_lo, Z_LO, (right,))
    layer_rows = layer_t.reshape(SEQ, mine * outer_here, inner_len)
    twiddle_high = twiddle.astype(BF)
    twiddle_low = (twiddle - twiddle_high.astype(F32)).astype(BF)
    twiddle_parts = jnp.concatenate([twiddle_high, twiddle_low], axis=0)
    twiddle_parts = jnp.broadcast_to(twiddle_parts, (SEQ,) + twiddle_parts.shape)
    right = gather("right_z", right, z_lo, Z_LO, 2)
    grad_rows = deliver("grad_z", grad_pieces, z_lo, Z_LO, 0)
    pre_send = after(hidden_pre.reshape(GROUP, quarter, hidden), grad_rows)
    pre_values = group_exchange("hidden_pre_z", pre_send)
    pre_values = pre_values.transpose(1, 0, 2).reshape(quarter, 4 * hidden)
    pre_values = lax.optimization_barrier(pre_values)
    right = gather("right_x", right, x, X, 1)

    grad_pieces = pieces_for(lambda other: part_of(grad_rows, other, 4, 1), y, Y)
    grad_blocks = deliver("grad_y", [p[None] for p in grad_pieces], y, Y, 0).astype(F32)
    left_down = down_left.astype(F32)
    down_mix = jnp.stack(
        [
            sum(left_down[j, k][:, None] * grad_blocks[j] for j in range(BLOCKS)).astype(BF)
            for k in range(BLOCKS)
        ]
    )
    down_pieces = pieces_for(
        lambda other: lax.dynamic_index_in_dim(down_mix, other, 0, keepdims=False), y, Y, (right,)
    )
    right = gather("right_core", right, core, CORE, 1)
    down_grad = deliver("down_y", down_pieces, y, Y, 1)

    layer_send = after(jnp.concatenate([layer_rows, twiddle_parts], axis=1), pre_values)
    layer_cols = seq_exchange("layer_seq", layer_send)

    def to_cols(value):
        return (
            value.reshape(SEQ, mine, outer_here, inner_len)
            .transpose(1, 0, 2, 3)
            .reshape(mine, outer_len, inner_len)
        )

    def to_rows(value):
        return (
            value.reshape(mine, SEQ, outer_here, inner_len)
            .transpose(1, 0, 2, 3)
            .reshape(SEQ, mine * outer_here, inner_len)
        )

    def blocks_to_cols(value, line):
        by_line = value.reshape(GROUP, 2, width // 2, quarter).transpose(1, 0, 2, 3)
        by_line = line_exchange("cols_z", by_line.reshape(8, width // 2, quarter))
        by_line, line = lax.optimization_barrier((by_line, line))
        by_line = by_line.reshape(2, GROUP, 8, mine, outer_here // GROUP, inner_len)
        by_line = by_line.transpose(2, 3, 0, 1, 4, 5).reshape(8, mine * 2 * outer_here, inner_len)
        by_plane = plane_exchange("cols_plane", by_line)
        by_plane = by_plane.reshape(8, mine, 2, outer_here, inner_len).transpose(1, 2, 0, 3, 4)
        return by_plane.reshape(mine, outer_len, inner_len), line

    def mixed_send(value):
        by_plane = value.reshape(mine, 2, 8, outer_here, inner_len).transpose(2, 0, 1, 3, 4)
        by_plane = plane_exchange("blocks_plane", by_plane.reshape(8, mine * 2 * outer_here, inner_len))
        return by_plane

    def mixed_arrive(by_plane):
        by_line = by_plane.reshape(width // 2, 2, outer_here, inner_len).transpose(1, 0, 2, 3)
        by_line = by_line.reshape(2, width // 2, GROUP, quarter).transpose(0, 2, 1, 3)
        by_line = by_line.reshape(8, width // 2, quarter)
        arrived = line_exchange("blocks_z", by_line)
        return arrived.reshape(2, GROUP, width // 2, quarter).transpose(1, 0, 2, 3).reshape(4 * width, quarter)

    layer_cols, twiddle_high, twiddle_low = jnp.split(
        layer_cols, [mine * outer_here, mine * outer_here + outer_here], axis=1
    )
    twiddle_all = (twiddle_high.astype(F32) + twiddle_low.astype(F32)).reshape(outer_len, inner_len)
    layer_cols = to_cols(layer_cols).astype(F32)
    key_mine = part_of(key_scale, seq, SEQ, 0)[:, None, None]
    query_mine = part_of(query_scale, seq, SEQ, 0)[:, None, None]
    key_input = (layer_cols * key_mine).astype(BF)
    first_pass = (
        jnp.einsum("bk,cak->cab", inner_tri, key_input, preferred_element_type=F32) * twiddle_all
    ).astype(BF)
    convolved = jnp.einsum("ij,cjb->cib", outer_tri, first_pass, preferred_element_type=F32).astype(BF)
    mixed = (layer_cols + layer_cols * query_mine * convolved.astype(F32)).astype(BF)
    mixed_plane = mixed_send(mixed)

    hidden_grad = jnp.einsum("pt,pq->tq", down_grad, right[0], preferred_element_type=F32)
    pre_f = pre_values.astype(F32)
    activated = jax.nn.gelu(pre_f).astype(BF)
    pre_grad = jax.vjp(jax.nn.gelu, pre_f)[1](hidden_grad)[0].astype(BF)
    down_terms = jnp.einsum("pt,tq->pq", down_grad, activated, preferred_element_type=F32)
    mix_pieces = pieces_for(lambda other: part_of(pre_grad, other, 4, 0)[None], y, Y)
    pre_blocks = deliver("pre_y", mix_pieces, y, Y, 0)
    pre_blocks = pre_blocks.astype(F32)
    left_up = up_left.astype(F32)
    right_mix = jnp.stack(
        [
            sum(left_up[j, k][None, :] * pre_blocks[j] for j in range(BLOCKS)).astype(BF)
            for k in range(BLOCKS)
        ]
    )
    right_pieces = pieces_for(
        lambda other: lax.dynamic_index_in_dim(right_mix, other, 0, keepdims=False), y, Y
    )
    seen = []
    right_grad = deliver("right_y", right_pieces, y, Y, 0, seen)
    mixed_rows = mixed_arrive(after(mixed_plane, seen[1]))
    partial_value = jnp.einsum("pq,tq->pt", right[1], right_grad, preferred_element_type=F32)
    mix_grad = (grad_rows.astype(F32) + partial_value).astype(BF)
    up_terms = jnp.einsum("pt,tq->pq", mixed_rows, right_grad, preferred_element_type=F32)
    weight_pair = weight_core(jnp.stack([down_terms, up_terms]), core)

    mix_grad, weight_sums = blocks_to_cols(mix_grad, weight_line(weight_pair, x))
    weight_sums = weight_z(weight_sums, z_lo)
    mix_grad, weight_sums = lax.optimization_barrier((mix_grad, weight_sums))
    weight_sums = weight_z_hi(weight_sums, z_hi)
    mix_grad = mix_grad.astype(F32)
    conv_f = convolved.astype(F32)
    grad_layer = mix_grad * layer_cols
    conv_grad = (grad_layer * query_mine).astype(BF)
    query_terms = jnp.sum(grad_layer * conv_f, axis=(1, 2))
    first_grad = jnp.einsum("ij,cib->cjb", outer_tri, conv_grad, preferred_element_type=F32).astype(BF)
    outer_terms = jnp.einsum("cib,cjb->ij", conv_grad, first_pass, preferred_element_type=F32)
    back_pass = (first_grad.astype(F32) * twiddle_all).astype(BF)
    key_grad = jnp.einsum("bk,cab->cak", inner_tri, back_pass, preferred_element_type=F32)
    inner_terms = jnp.einsum("cab,cak->bk", back_pass, key_input, preferred_element_type=F32)
    key_terms = jnp.sum(key_grad * layer_cols, axis=(1, 2))
    grad_input = (mix_grad * (1.0 + query_mine * conv_f) + key_mine * key_grad).astype(BF)
    grad_input = seq_exchange("grad_input_seq", to_rows(grad_input))

    side = 128
    count = inner_len // side
    tiles = [
        inner_terms[i * side : (i + 1) * side, j * side : (j + 1) * side]
        for i in range(count)
        for j in range(i + 1)
    ]
    model = CHAN * width
    at = chan * width + seq * mine
    scales = jnp.zeros((2, model), F32)
    scales = lax.dynamic_update_slice(scales, jnp.stack([query_terms, key_terms]), (0, at))
    scale_rows = 2 * model // side
    sums = jnp.concatenate(tiles + [outer_terms, scales.reshape(scale_rows, side)], axis=0)
    whole_rows = -(-sums.shape[0] // 512) * 512
    sums = jnp.pad(sums, ((0, whole_rows - sums.shape[0]), (0, 0)))
    sums, weight_sums = lax.optimization_barrier((sums, weight_sums))
    for me, masks in ((y, Y), (z_lo, Z_LO)):
        sums = sum_spread_f32("sums", lambda other, sums=sums: part_of(sums, other, 4, 0), me, masks)
    sums = sum_spread_f32("sums", lambda other, sums=sums: sums, x, X)
    sums, grad_input = lax.optimization_barrier((sums, grad_input))
    sums = sum_spread_f32("sums", lambda other, sums=sums: sums, x, join(Z_HI, CORE))
    for me, masks in ((z_lo, Z_LO), (y, Y)):
        sums = gather("sums_back", sums, me, masks, 0)
    blank = jnp.zeros((side, side), F32)
    rows, taken = [], 0
    for i in range(count):
        rows.append(
            jnp.concatenate(
                [sums[(taken + j) * side : (taken + j + 1) * side] for j in range(i + 1)]
                + [blank] * (count - 1 - i),
                axis=1,
            )
        )
        taken += i + 1
    inner_total = jnp.where(inner_mask, jnp.concatenate(rows, axis=0), 0.0)
    outer_total = jnp.where(outer_mask, sums[taken * side : (taken + 1) * side], 0.0)
    scale_total = sums[(taken + 1) * side : (taken + 1) * side + scale_rows].reshape(2, model)
    scale_total = lax.dynamic_slice_in_dim(scale_total, chan * width, width, 1)

    token_scale = (SEQ * tokens) ** (-0.5)
    weights = weight_sums * token_scale
    grad_down, grad_up = weights[0], weights[1].T
    return (
        grad_input.reshape(width, tokens).T,
        grad_up[None],
        grad_down[None],
        scale_total[0] * token_scale,
        scale_total[1] * token_scale,
        inner_total * (outer_len * model) ** (-0.5),
        outer_total * (inner_len * model) ** (-0.5),
    )


def solution(mesh):
    return jax.shard_map(
        body,
        mesh=mesh,
        in_specs=(
            P("seq", "chan"),
            P("chan"),
            P("chan"),
            P("seq", None),
            P(),
            P(),
            P("seq", "chan"),
            P("seq", "chan"),
            P("chan", None, None),
            P(),
            P("chan", None, None),
            P(),
        ),
        out_specs=(
            P("seq", "chan"),
            P("chan", None, "seq"),
            P("chan", "seq", None),
            P("chan"),
            P("chan"),
            P(),
            P(),
        ),
        check_vma=False,
    )
```

```python
import jax
import jax.numpy as jnp
from jax import lax
from jax.sharding import PartitionSpec as P

BF = jnp.bfloat16
F32 = jnp.float32
BLOCKS = 4
GROUP = 4
SEQ = 16
CHAN = 16
Z_LO = [0, 1, 2, 3]
Y = [0, 4, 8, 12]
CORE = [0, 16]
X = [0, 32, 64, 96]
Z_HI = [0, 128]


def join(high, low):
    return [h ^ l for h in high for l in low]


def swap(value, mask):
    if mask == 0:
        return value
    route = [(i, i ^ mask) for i in range(SEQ * CHAN)]
    return lax.ppermute(value, ("seq", "chan"), route)


def pieces_for(take, me, masks, behind=()):
    pieces = [take(jnp.bitwise_xor(me, step)) for step in range(len(masks))]
    return list(lax.optimization_barrier((*pieces, *behind))[: len(masks)])


def deliver(name, pieces, me, masks, axis):
    size = pieces[0].shape[axis]
    shape = list(pieces[0].shape)
    shape[axis] = size * len(masks)
    out = jnp.zeros(shape, pieces[0].dtype)
    for step, mask in enumerate(masks):
        with jax.named_scope(name):
            arrived = swap(pieces[step], mask)
        out = lax.dynamic_update_slice_in_dim(out, arrived, jnp.bitwise_xor(me, step) * size, axis)
    return out


def after(value, *others):
    return lax.optimization_barrier((value, *others))[0]


def part_of(value, index, count, axis):
    size = value.shape[axis] // count
    return lax.dynamic_slice_in_dim(value, index * size, size, axis)


def sum_spread(name, take, me, masks):
    total = None
    for step, mask in enumerate(masks):
        piece = take(jnp.bitwise_xor(me, step))
        with jax.named_scope(name):
            arrived = swap(piece.astype(BF), mask).astype(F32) if mask else piece.astype(F32)
        total = arrived if total is None else total + arrived
    return total


def sum_spread_f32(name, take, me, masks):
    total = None
    for step, mask in enumerate(masks):
        with jax.named_scope(name):
            arrived = swap(take(jnp.bitwise_xor(me, step)), mask)
        total = arrived if total is None else total + arrived
    return total


def gather(name, value, me, masks, axis):
    return deliver(name, [value] * len(masks), me, masks, axis)


def seq_exchange(name, value):
    with jax.named_scope(name):
        return lax.all_to_all(value, "seq", split_axis=0, concat_axis=0, tiled=True)


def plane_exchange(name, value):
    groups = [list(range(8)), list(range(8, SEQ))]
    with jax.named_scope(name):
        return lax.all_to_all(
            value, "seq", split_axis=0, concat_axis=0, axis_index_groups=groups, tiled=True
        )


def group_exchange(name, value):
    groups = [list(range(first, first + GROUP)) for first in range(0, CHAN, GROUP)]
    with jax.named_scope(name):
        return lax.all_to_all(
            value, "chan", split_axis=0, concat_axis=0, axis_index_groups=groups, tiled=True
        )


def line_exchange(name, value):
    groups = [
        [(z_hi * 8 + plane) * CHAN + block * GROUP + z_lo for z_hi in range(2) for z_lo in range(GROUP)]
        for plane in range(8)
        for block in range(BLOCKS)
    ]
    with jax.named_scope(name):
        return lax.all_to_all(
            value, ("seq", "chan"), split_axis=0, concat_axis=0, axis_index_groups=groups, tiled=True
        )


def lower_mask(size):
    return jnp.arange(size)[:, None] >= jnp.arange(size)[None, :]


def weight_core(terms, core):
    count, rows, width = terms.shape
    split = terms.reshape(count, 8, 2, rows // 16, width)
    pair = sum_spread(
        "weight_core", lambda other: lax.dynamic_index_in_dim(split, other, 2, keepdims=False), core, CORE
    )
    return pair.reshape(count, 2, 4, rows // 16, width)


def weight_line(pair, x):
    return sum_spread(
        "weight_x", lambda other: lax.dynamic_index_in_dim(pair, other, 2, keepdims=False), x, X
    )


def weight_z(line, z_lo):
    return sum_spread("weight_z", lambda other: part_of(line, other, 4, 3), z_lo, Z_LO)


def weight_z_hi(line, z_hi):
    return sum_spread(
        "weight_z_hi", lambda other: lax.dynamic_index_in_dim(line, other, 1, keepdims=False), z_hi, Z_HI
    )


def body(
    layer_input,
    query_scale,
    key_scale,
    twiddle,
    seq_inner,
    seq_outer,
    grad_output,
    hidden_pre,
    up_right,
    up_left,
    down_right,
    down_left,
):
    outer_here, inner_len = twiddle.shape
    tokens, width = layer_input.shape
    outer_len = seq_outer.shape[0]
    hidden = hidden_pre.shape[1]
    quarter = tokens // GROUP
    seq = lax.axis_index("seq")
    chan = lax.axis_index("chan")
    z_lo, y = chan % 4, chan // 4
    core, x, z_hi = seq % 2, (seq // 2) % 4, seq // 8
    mine = width // SEQ
    inner_mask = lower_mask(inner_len)
    outer_mask = lower_mask(outer_len)
    inner_tri = jnp.where(inner_mask, seq_inner, jnp.zeros_like(seq_inner))
    outer_tri = jnp.where(outer_mask, seq_outer, jnp.zeros_like(seq_outer))
    layer_t = layer_input.T
    grad_t = grad_output.T
    piece = quarter // BLOCKS

    right = jnp.stack([down_right[0], up_right[0].T])
    right = part_of(right, core * 4 + x, 8, 1)

    grad_pieces = pieces_for(lambda other: part_of(grad_t, other, 4, 1), z_lo, Z_LO, (right,))
    layer_rows = layer_t.reshape(SEQ, mine * outer_here, inner_len)
    twiddle_high = twiddle.astype(BF)
    twiddle_low = (twiddle - twiddle_high.astype(F32)).astype(BF)
    twiddle_parts = jnp.concatenate([twiddle_high, twiddle_low], axis=0)
    twiddle_parts = jnp.broadcast_to(twiddle_parts, (SEQ,) + twiddle_parts.shape)
    right = gather("right_z", right, z_lo, Z_LO, 2)
    grad_rows = deliver("grad_z", grad_pieces, z_lo, Z_LO, 0)
    pre_send = after(hidden_pre.reshape(GROUP, quarter, hidden), grad_rows, right)
    pre_values = group_exchange("hidden_pre_z", pre_send)
    pre_values = pre_values.transpose(1, 0, 2).reshape(quarter, 4 * hidden)
    pre_values = lax.optimization_barrier(pre_values)
    right = gather("right_x", right, x, X, 1)

    grad_pieces = pieces_for(lambda other: part_of(grad_rows, other, 4, 1), y, Y)
    grad_blocks = deliver("grad_y", [p[None] for p in grad_pieces], y, Y, 0).astype(F32)
    left_down = down_left.astype(F32)
    down_mix = jnp.stack(
        [
            sum(left_down[j, k][:, None] * grad_blocks[j] for j in range(BLOCKS)).astype(BF)
            for k in range(BLOCKS)
        ]
    )
    down_pieces = pieces_for(
        lambda other: lax.dynamic_index_in_dim(down_mix, other, 0, keepdims=False), y, Y, (right,)
    )
    right = gather("right_core", right, core, CORE, 1)
    down_grad = deliver("down_y", down_pieces, y, Y, 1)

    layer_send = after(jnp.concatenate([layer_rows, twiddle_parts], axis=1), pre_values)
    layer_cols = seq_exchange("layer_seq", layer_send)

    def to_cols(value):
        return (
            value.reshape(SEQ, mine, outer_here, inner_len)
            .transpose(1, 0, 2, 3)
            .reshape(mine, outer_len, inner_len)
        )

    def to_rows(value):
        return (
            value.reshape(mine, SEQ, outer_here, inner_len)
            .transpose(1, 0, 2, 3)
            .reshape(SEQ, mine * outer_here, inner_len)
        )

    def blocks_to_cols(value):
        by_line = value.reshape(GROUP, 2, width // 2, quarter).transpose(1, 0, 2, 3)
        by_line = line_exchange("cols_z", by_line.reshape(8, width // 2, quarter))
        by_line = by_line.reshape(2, GROUP, 8, mine, outer_here // GROUP, inner_len)
        by_line = by_line.transpose(2, 3, 0, 1, 4, 5).reshape(8, mine * 2 * outer_here, inner_len)
        by_plane = plane_exchange("cols_plane", by_line)
        by_plane = by_plane.reshape(8, mine, 2, outer_here, inner_len).transpose(1, 2, 0, 3, 4)
        return by_plane.reshape(mine, outer_len, inner_len)

    def mixed_send(value):
        by_plane = value.reshape(mine, 2, 8, outer_here, inner_len).transpose(2, 0, 1, 3, 4)
        by_plane = plane_exchange("blocks_plane", by_plane.reshape(8, mine * 2 * outer_here, inner_len))
        return by_plane

    def mixed_arrive(by_plane):
        by_line = by_plane.reshape(width // 2, 2, outer_here, inner_len).transpose(1, 0, 2, 3)
        by_line = by_line.reshape(2, width // 2, GROUP, quarter).transpose(0, 2, 1, 3)
        by_line = by_line.reshape(8, width // 2, quarter)
        arrived = line_exchange("blocks_z", by_line)
        return arrived.reshape(2, GROUP, width // 2, quarter).transpose(1, 0, 2, 3).reshape(4 * width, quarter)

    layer_cols, twiddle_high, twiddle_low = jnp.split(
        layer_cols, [mine * outer_here, mine * outer_here + outer_here], axis=1
    )
    twiddle_all = (twiddle_high.astype(F32) + twiddle_low.astype(F32)).reshape(outer_len, inner_len)
    layer_cols = to_cols(layer_cols).astype(F32)
    key_mine = part_of(key_scale, seq, SEQ, 0)[:, None, None]
    query_mine = part_of(query_scale, seq, SEQ, 0)[:, None, None]
    key_input = (layer_cols * key_mine).astype(BF)
    first_pass = (
        jnp.einsum("bk,cak->cab", inner_tri, key_input, preferred_element_type=F32) * twiddle_all
    ).astype(BF)
    convolved = jnp.einsum("ij,cjb->cib", outer_tri, first_pass, preferred_element_type=F32).astype(BF)
    mixed = (layer_cols + layer_cols * query_mine * convolved.astype(F32)).astype(BF)
    mixed_plane = mixed_send(mixed)

    hidden_grad = jnp.einsum("pt,pq->tq", down_grad, right[0], preferred_element_type=F32)
    pre_f = pre_values.astype(F32)
    activated = jax.nn.gelu(pre_f).astype(BF)
    pre_grad = jax.vjp(jax.nn.gelu, pre_f)[1](hidden_grad)[0].astype(BF)
    down_terms = jnp.einsum("pt,tq->pq", down_grad, activated, preferred_element_type=F32)
    mix_pieces = pieces_for(lambda other: part_of(pre_grad, other, 4, 0)[None], y, Y)
    pre_blocks = deliver("pre_y", mix_pieces, y, Y, 0)
    pre_blocks = pre_blocks.astype(F32)
    left_up = up_left.astype(F32)
    right_mix = jnp.stack(
        [
            sum(left_up[j, k][None, :] * pre_blocks[j] for j in range(BLOCKS)).astype(BF)
            for k in range(BLOCKS)
        ]
    )
    right_pieces = pieces_for(
        lambda other: lax.dynamic_index_in_dim(right_mix, other, 0, keepdims=False), y, Y
    )
    right_grad = deliver("right_y", right_pieces, y, Y, 0)
    partial_value = jnp.einsum("pq,tq->pt", right[1], right_grad, preferred_element_type=F32)
    mix_grad = (grad_rows.astype(F32) + partial_value).astype(BF)

    mix_grad = blocks_to_cols(mix_grad)
    mixed_rows = mixed_arrive(after(mixed_plane, mix_grad))
    up_terms = jnp.einsum("pt,tq->pq", mixed_rows, right_grad, preferred_element_type=F32)
    weight_sums = weight_core(jnp.stack([down_terms, up_terms]), core)
    mix_grad = mix_grad.astype(F32)
    conv_f = convolved.astype(F32)
    grad_layer = mix_grad * layer_cols
    conv_grad = (grad_layer * query_mine).astype(BF)
    query_terms = jnp.sum(grad_layer * conv_f, axis=(1, 2))
    first_grad = jnp.einsum("ij,cib->cjb", outer_tri, conv_grad, preferred_element_type=F32).astype(BF)
    outer_terms = jnp.einsum("cib,cjb->ij", conv_grad, first_pass, preferred_element_type=F32)
    back_pass = (first_grad.astype(F32) * twiddle_all).astype(BF)
    key_grad = jnp.einsum("bk,cab->cak", inner_tri, back_pass, preferred_element_type=F32)
    inner_terms = jnp.einsum("cab,cak->bk", back_pass, key_input, preferred_element_type=F32)
    key_terms = jnp.sum(key_grad * layer_cols, axis=(1, 2))
    grad_input = (mix_grad * (1.0 + query_mine * conv_f) + key_mine * key_grad).astype(BF)
    grad_input = seq_exchange("grad_input_seq", to_rows(grad_input))

    side = 128
    count = inner_len // side
    tiles = [
        inner_terms[i * side : (i + 1) * side, j * side : (j + 1) * side]
        for i in range(count)
        for j in range(i + 1)
    ]
    model = CHAN * width
    at = chan * width + seq * mine
    scales = jnp.zeros((2, model), F32)
    scales = lax.dynamic_update_slice(scales, jnp.stack([query_terms, key_terms]), (0, at))
    scale_rows = 2 * model // side
    sums = jnp.concatenate(tiles + [outer_terms, scales.reshape(scale_rows, side)], axis=0)
    whole_rows = -(-sums.shape[0] // 512) * 512
    sums = jnp.pad(sums, ((0, whole_rows - sums.shape[0]), (0, 0)))
    for me, masks in ((y, Y), (z_lo, Z_LO)):
        sums = sum_spread_f32("sums", lambda other, sums=sums: part_of(sums, other, 4, 0), me, masks)
    sums = sum_spread_f32("sums", lambda other, sums=sums: sums, x, X)
    sums, weight_sums = lax.optimization_barrier((sums, weight_sums))
    weight_sums = weight_line(weight_sums, x)
    sums = sum_spread_f32("sums", lambda other, sums=sums: sums, x, join(Z_HI, CORE))
    sums, weight_sums, grad_input = lax.optimization_barrier((sums, weight_sums, grad_input))
    weight_sums = weight_z(weight_sums, z_lo)
    sums = gather("sums_back", sums, z_lo, Z_LO, 0)
    sums, weight_sums = lax.optimization_barrier((sums, weight_sums))
    weight_sums = weight_z_hi(weight_sums, z_hi)
    sums = gather("sums_back", sums, y, Y, 0)
    blank = jnp.zeros((side, side), F32)
    rows, taken = [], 0
    for i in range(count):
        rows.append(
            jnp.concatenate(
                [sums[(taken + j) * side : (taken + j + 1) * side] for j in range(i + 1)]
                + [blank] * (count - 1 - i),
                axis=1,
            )
        )
        taken += i + 1
    inner_total = jnp.where(inner_mask, jnp.concatenate(rows, axis=0), 0.0)
    outer_total = jnp.where(outer_mask, sums[taken * side : (taken + 1) * side], 0.0)
    scale_total = sums[(taken + 1) * side : (taken + 1) * side + scale_rows].reshape(2, model)
    scale_total = lax.dynamic_slice_in_dim(scale_total, chan * width, width, 1)

    token_scale = (SEQ * tokens) ** (-0.5)
    weights = weight_sums * token_scale
    grad_down, grad_up = weights[0], weights[1].T
    return (
        grad_input.reshape(width, tokens).T,
        grad_up[None],
        grad_down[None],
        scale_total[0] * token_scale,
        scale_total[1] * token_scale,
        inner_total * (outer_len * model) ** (-0.5),
        outer_total * (inner_len * model) ** (-0.5),
    )


def solution(mesh):
    return jax.shard_map(
        body,
        mesh=mesh,
        in_specs=(
            P("seq", "chan"),
            P("chan"),
            P("chan"),
            P("seq", None),
            P(),
            P(),
            P("seq", "chan"),
            P("seq", "chan"),
            P("chan", None, None),
            P(),
            P("chan", None, None),
            P(),
        ),
        out_specs=(
            P("seq", "chan"),
            P("chan", None, "seq"),
            P("chan", "seq", None),
            P("chan"),
            P("chan"),
            P(),
            P(),
        ),
        check_vma=False,
    )
```

```python
import jax
import jax.numpy as jnp
from jax import lax
from jax.sharding import PartitionSpec as P

BF = jnp.bfloat16
F32 = jnp.float32
BLOCKS = 4
GROUP = 4
SEQ = 16
CHAN = 16
Z_LO = [0, 1, 2, 3]
Y = [0, 4, 8, 12]
CORE = [0, 16]
X = [0, 32, 64, 96]
Z_HI = [0, 128]


def join(high, low):
    return [h ^ l for h in high for l in low]


def swap(value, mask):
    if mask == 0:
        return value
    route = [(i, i ^ mask) for i in range(SEQ * CHAN)]
    return lax.ppermute(value, ("seq", "chan"), route)


def pieces_for(take, me, masks, behind=()):
    pieces = [take(jnp.bitwise_xor(me, step)) for step in range(len(masks))]
    return list(lax.optimization_barrier((*pieces, *behind))[: len(masks)])


def deliver(name, pieces, me, masks, axis):
    size = pieces[0].shape[axis]
    shape = list(pieces[0].shape)
    shape[axis] = size * len(masks)
    out = jnp.zeros(shape, pieces[0].dtype)
    for step, mask in enumerate(masks):
        with jax.named_scope(name):
            arrived = swap(pieces[step], mask)
        out = lax.dynamic_update_slice_in_dim(out, arrived, jnp.bitwise_xor(me, step) * size, axis)
    return out


def after(value, *others):
    return lax.optimization_barrier((value, *others))[0]


def part_of(value, index, count, axis):
    size = value.shape[axis] // count
    return lax.dynamic_slice_in_dim(value, index * size, size, axis)


def sum_spread(name, take, me, masks):
    total = None
    for step, mask in enumerate(masks):
        piece = take(jnp.bitwise_xor(me, step))
        with jax.named_scope(name):
            arrived = swap(piece.astype(BF), mask).astype(F32) if mask else piece.astype(F32)
        total = arrived if total is None else total + arrived
    return total


def sum_spread_f32(name, take, me, masks):
    total = None
    for step, mask in enumerate(masks):
        with jax.named_scope(name):
            arrived = swap(take(jnp.bitwise_xor(me, step)), mask)
        total = arrived if total is None else total + arrived
    return total


def gather(name, value, me, masks, axis):
    return deliver(name, [value] * len(masks), me, masks, axis)


def seq_exchange(name, value):
    with jax.named_scope(name):
        return lax.all_to_all(value, "seq", split_axis=0, concat_axis=0, tiled=True)


def plane_exchange(name, value):
    groups = [list(range(8)), list(range(8, SEQ))]
    with jax.named_scope(name):
        return lax.all_to_all(
            value, "seq", split_axis=0, concat_axis=0, axis_index_groups=groups, tiled=True
        )


def group_exchange(name, value):
    groups = [list(range(first, first + GROUP)) for first in range(0, CHAN, GROUP)]
    with jax.named_scope(name):
        return lax.all_to_all(
            value, "chan", split_axis=0, concat_axis=0, axis_index_groups=groups, tiled=True
        )


def line_exchange(name, value):
    groups = [
        [(z_hi * 8 + plane) * CHAN + block * GROUP + z_lo for z_hi in range(2) for z_lo in range(GROUP)]
        for plane in range(8)
        for block in range(BLOCKS)
    ]
    with jax.named_scope(name):
        return lax.all_to_all(
            value, ("seq", "chan"), split_axis=0, concat_axis=0, axis_index_groups=groups, tiled=True
        )


def lower_mask(size):
    return jnp.arange(size)[:, None] >= jnp.arange(size)[None, :]


def weight_core(terms, core):
    count, rows, width = terms.shape
    split = terms.reshape(count, 8, 2, rows // 16, width)
    pair = sum_spread(
        "weight_core", lambda other: lax.dynamic_index_in_dim(split, other, 2, keepdims=False), core, CORE
    )
    return pair.reshape(count, 2, 4, rows // 16, width)


def weight_line(pair, x):
    return sum_spread(
        "weight_x", lambda other: lax.dynamic_index_in_dim(pair, other, 2, keepdims=False), x, X
    )


def weight_z(line, z_lo):
    return sum_spread("weight_z", lambda other: part_of(line, other, 4, 3), z_lo, Z_LO)


def weight_z_hi(line, z_hi):
    return sum_spread(
        "weight_z_hi", lambda other: lax.dynamic_index_in_dim(line, other, 1, keepdims=False), z_hi, Z_HI
    )


def body(
    layer_input,
    query_scale,
    key_scale,
    twiddle,
    seq_inner,
    seq_outer,
    grad_output,
    hidden_pre,
    up_right,
    up_left,
    down_right,
    down_left,
):
    outer_here, inner_len = twiddle.shape
    tokens, width = layer_input.shape
    outer_len = seq_outer.shape[0]
    hidden = hidden_pre.shape[1]
    quarter = tokens // GROUP
    seq = lax.axis_index("seq")
    chan = lax.axis_index("chan")
    z_lo, y = chan % 4, chan // 4
    core, x, z_hi = seq % 2, (seq // 2) % 4, seq // 8
    mine = width // SEQ
    inner_mask = lower_mask(inner_len)
    outer_mask = lower_mask(outer_len)
    inner_tri = jnp.where(inner_mask, seq_inner, jnp.zeros_like(seq_inner))
    outer_tri = jnp.where(outer_mask, seq_outer, jnp.zeros_like(seq_outer))
    layer_t = layer_input.T
    grad_t = grad_output.T
    piece = quarter // BLOCKS

    right = jnp.stack([down_right[0], up_right[0].T])
    right = part_of(right, core * 4 + x, 8, 1)

    grad_pieces = pieces_for(lambda other: part_of(grad_t, other, 4, 1), z_lo, Z_LO, (right,))
    layer_rows = layer_t.reshape(SEQ, mine * outer_here, inner_len)
    twiddle_high = twiddle.astype(BF)
    twiddle_low = (twiddle - twiddle_high.astype(F32)).astype(BF)
    twiddle_parts = jnp.concatenate([twiddle_high, twiddle_low], axis=0)
    twiddle_parts = jnp.broadcast_to(twiddle_parts, (SEQ,) + twiddle_parts.shape)
    right = gather("right_z", right, z_lo, Z_LO, 2)
    grad_rows = deliver("grad_z", grad_pieces, z_lo, Z_LO, 0)
    pre_send = after(hidden_pre.reshape(GROUP, quarter, hidden), grad_rows, right)
    pre_values = group_exchange("hidden_pre_z", pre_send)
    pre_values = pre_values.transpose(1, 0, 2).reshape(quarter, 4 * hidden)
    pre_values = lax.optimization_barrier(pre_values)
    right = gather("right_x", right, x, X, 1)

    grad_pieces = pieces_for(lambda other: part_of(grad_rows, other, 4, 1), y, Y)
    grad_blocks = deliver("grad_y", [p[None] for p in grad_pieces], y, Y, 0).astype(F32)
    left_down = down_left.astype(F32)
    down_mix = jnp.stack(
        [
            sum(left_down[j, k][:, None] * grad_blocks[j] for j in range(BLOCKS)).astype(BF)
            for k in range(BLOCKS)
        ]
    )
    down_pieces = pieces_for(
        lambda other: lax.dynamic_index_in_dim(down_mix, other, 0, keepdims=False), y, Y, (right,)
    )
    right = gather("right_core", right, core, CORE, 1)
    down_grad = deliver("down_y", down_pieces, y, Y, 1)

    layer_send = after(jnp.concatenate([layer_rows, twiddle_parts], axis=1), pre_values)
    layer_cols = seq_exchange("layer_seq", layer_send)

    def to_cols(value):
        return (
            value.reshape(SEQ, mine, outer_here, inner_len)
            .transpose(1, 0, 2, 3)
            .reshape(mine, outer_len, inner_len)
        )

    def to_rows(value):
        return (
            value.reshape(mine, SEQ, outer_here, inner_len)
            .transpose(1, 0, 2, 3)
            .reshape(SEQ, mine * outer_here, inner_len)
        )

    def blocks_to_cols(value):
        by_line = value.reshape(GROUP, 2, width // 2, quarter).transpose(1, 0, 2, 3)
        by_line = line_exchange("cols_z", by_line.reshape(8, width // 2, quarter))
        by_line = by_line.reshape(2, GROUP, 8, mine, outer_here // GROUP, inner_len)
        by_line = by_line.transpose(2, 3, 0, 1, 4, 5).reshape(8, mine * 2 * outer_here, inner_len)
        by_plane = plane_exchange("cols_plane", by_line)
        by_plane = by_plane.reshape(8, mine, 2, outer_here, inner_len).transpose(1, 2, 0, 3, 4)
        return by_plane.reshape(mine, outer_len, inner_len)

    def mixed_send(value):
        by_plane = value.reshape(mine, 2, 8, outer_here, inner_len).transpose(2, 0, 1, 3, 4)
        by_plane = plane_exchange("blocks_plane", by_plane.reshape(8, mine * 2 * outer_here, inner_len))
        return by_plane

    def mixed_arrive(by_plane):
        by_line = by_plane.reshape(width // 2, 2, outer_here, inner_len).transpose(1, 0, 2, 3)
        by_line = by_line.reshape(2, width // 2, GROUP, quarter).transpose(0, 2, 1, 3)
        by_line = by_line.reshape(8, width // 2, quarter)
        arrived = line_exchange("blocks_z", by_line)
        return arrived.reshape(2, GROUP, width // 2, quarter).transpose(1, 0, 2, 3).reshape(4 * width, quarter)

    layer_cols, twiddle_high, twiddle_low = jnp.split(
        layer_cols, [mine * outer_here, mine * outer_here + outer_here], axis=1
    )
    twiddle_all = (twiddle_high.astype(F32) + twiddle_low.astype(F32)).reshape(outer_len, inner_len)
    layer_cols = to_cols(layer_cols).astype(F32)
    key_mine = part_of(key_scale, seq, SEQ, 0)[:, None, None]
    query_mine = part_of(query_scale, seq, SEQ, 0)[:, None, None]
    key_input = (layer_cols * key_mine).astype(BF)
    first_pass = (
        jnp.einsum("bk,cak->cab", inner_tri, key_input, preferred_element_type=F32) * twiddle_all
    ).astype(BF)
    convolved = jnp.einsum("ij,cjb->cib", outer_tri, first_pass, preferred_element_type=F32).astype(BF)
    mixed = (layer_cols + layer_cols * query_mine * convolved.astype(F32)).astype(BF)
    mixed_plane = mixed_send(mixed)

    hidden_grad = jnp.einsum("pt,pq->tq", down_grad, right[0], preferred_element_type=F32)
    pre_f = pre_values.astype(F32)
    activated = jax.nn.gelu(pre_f).astype(BF)
    pre_grad = jax.vjp(jax.nn.gelu, pre_f)[1](hidden_grad)[0].astype(BF)
    down_terms = jnp.einsum("pt,tq->pq", down_grad, activated, preferred_element_type=F32)
    mix_pieces = pieces_for(lambda other: part_of(pre_grad, other, 4, 0)[None], y, Y)
    pre_blocks = deliver("pre_y", mix_pieces, y, Y, 0)
    pre_blocks = pre_blocks.astype(F32)
    left_up = up_left.astype(F32)
    right_mix = jnp.stack(
        [
            sum(left_up[j, k][None, :] * pre_blocks[j] for j in range(BLOCKS)).astype(BF)
            for k in range(BLOCKS)
        ]
    )
    right_pieces = pieces_for(
        lambda other: lax.dynamic_index_in_dim(right_mix, other, 0, keepdims=False), y, Y
    )
    right_grad = deliver("right_y", right_pieces, y, Y, 0)
    right_grad, mixed_plane = lax.optimization_barrier((right_grad, mixed_plane))
    partial_value = jnp.einsum("pq,tq->pt", right[1], right_grad, preferred_element_type=F32)
    mix_grad = (grad_rows.astype(F32) + partial_value).astype(BF)

    mix_grad = blocks_to_cols(mix_grad)
    mixed_rows = mixed_arrive(after(mixed_plane, mix_grad))
    up_terms = jnp.einsum("pt,tq->pq", mixed_rows, right_grad, preferred_element_type=F32)
    weight_sums = weight_core(jnp.stack([down_terms, up_terms]), core)
    mix_grad = mix_grad.astype(F32)
    conv_f = convolved.astype(F32)
    grad_layer = mix_grad * layer_cols
    conv_grad = (grad_layer * query_mine).astype(BF)
    query_terms = jnp.sum(grad_layer * conv_f, axis=(1, 2))
    first_grad = jnp.einsum("ij,cib->cjb", outer_tri, conv_grad, preferred_element_type=F32).astype(BF)
    outer_terms = jnp.einsum("cib,cjb->ij", conv_grad, first_pass, preferred_element_type=F32)
    back_pass = (first_grad.astype(F32) * twiddle_all).astype(BF)
    key_grad = jnp.einsum("bk,cab->cak", inner_tri, back_pass, preferred_element_type=F32)
    inner_terms = jnp.einsum("cab,cak->bk", back_pass, key_input, preferred_element_type=F32)
    key_terms = jnp.sum(key_grad * layer_cols, axis=(1, 2))
    grad_input = (mix_grad * (1.0 + query_mine * conv_f) + key_mine * key_grad).astype(BF)
    grad_input = seq_exchange("grad_input_seq", to_rows(grad_input))

    side = 128
    count = inner_len // side
    tiles = [
        inner_terms[i * side : (i + 1) * side, j * side : (j + 1) * side]
        for i in range(count)
        for j in range(i + 1)
    ]
    model = CHAN * width
    at = chan * width + seq * mine
    scales = jnp.zeros((2, model), F32)
    scales = lax.dynamic_update_slice(scales, jnp.stack([query_terms, key_terms]), (0, at))
    scale_rows = 2 * model // side
    sums = jnp.concatenate(tiles + [outer_terms, scales.reshape(scale_rows, side)], axis=0)
    whole_rows = -(-sums.shape[0] // 512) * 512
    sums = jnp.pad(sums, ((0, whole_rows - sums.shape[0]), (0, 0)))
    for me, masks in ((y, Y), (z_lo, Z_LO)):
        sums = sum_spread_f32("sums", lambda other, sums=sums: part_of(sums, other, 4, 0), me, masks)
    sums = sum_spread_f32("sums", lambda other, sums=sums: sums, x, X)
    sums, weight_sums = lax.optimization_barrier((sums, weight_sums))
    weight_sums = weight_line(weight_sums, x)
    sums = sum_spread_f32("sums", lambda other, sums=sums: sums, x, join(Z_HI, CORE))
    sums, weight_sums, grad_input = lax.optimization_barrier((sums, weight_sums, grad_input))
    weight_sums = weight_z(weight_sums, z_lo)
    sums = gather("sums_back", sums, z_lo, Z_LO, 0)
    sums, weight_sums = lax.optimization_barrier((sums, weight_sums))
    weight_sums = weight_z_hi(weight_sums, z_hi)
    sums = gather("sums_back", sums, y, Y, 0)
    blank = jnp.zeros((side, side), F32)
    rows, taken = [], 0
    for i in range(count):
        rows.append(
            jnp.concatenate(
                [sums[(taken + j) * side : (taken + j + 1) * side] for j in range(i + 1)]
                + [blank] * (count - 1 - i),
                axis=1,
            )
        )
        taken += i + 1
    inner_total = jnp.where(inner_mask, jnp.concatenate(rows, axis=0), 0.0)
    outer_total = jnp.where(outer_mask, sums[taken * side : (taken + 1) * side], 0.0)
    scale_total = sums[(taken + 1) * side : (taken + 1) * side + scale_rows].reshape(2, model)
    scale_total = lax.dynamic_slice_in_dim(scale_total, chan * width, width, 1)

    token_scale = (SEQ * tokens) ** (-0.5)
    weights = weight_sums * token_scale
    grad_down, grad_up = weights[0], weights[1].T
    return (
        grad_input.reshape(width, tokens).T,
        grad_up[None],
        grad_down[None],
        scale_total[0] * token_scale,
        scale_total[1] * token_scale,
        inner_total * (outer_len * model) ** (-0.5),
        outer_total * (inner_len * model) ** (-0.5),
    )


def solution(mesh):
    return jax.shard_map(
        body,
        mesh=mesh,
        in_specs=(
            P("seq", "chan"),
            P("chan"),
            P("chan"),
            P("seq", None),
            P(),
            P(),
            P("seq", "chan"),
            P("seq", "chan"),
            P("chan", None, None),
            P(),
            P("chan", None, None),
            P(),
        ),
        out_specs=(
            P("seq", "chan"),
            P("chan", None, "seq"),
            P("chan", "seq", None),
            P("chan"),
            P("chan"),
            P(),
            P(),
        ),
        check_vma=False,
    )
```

```python
import jax
import jax.numpy as jnp
from jax import lax
from jax.sharding import PartitionSpec as P

BF = jnp.bfloat16
F32 = jnp.float32
BLOCKS = 4
GROUP = 4
SEQ = 16
CHAN = 16
Z_LO = [0, 1, 2, 3]
Y = [0, 4, 8, 12]
CORE = [0, 16]
X = [0, 32, 64, 96]
Z_HI = [0, 128]


def join(high, low):
    return [h ^ l for h in high for l in low]


def swap(value, mask):
    if mask == 0:
        return value
    route = [(i, i ^ mask) for i in range(SEQ * CHAN)]
    return lax.ppermute(value, ("seq", "chan"), route)


def pieces_for(take, me, masks, behind=()):
    pieces = [take(jnp.bitwise_xor(me, step)) for step in range(len(masks))]
    return list(lax.optimization_barrier((*pieces, *behind))[: len(masks)])


def deliver(name, pieces, me, masks, axis):
    size = pieces[0].shape[axis]
    shape = list(pieces[0].shape)
    shape[axis] = size * len(masks)
    out = jnp.zeros(shape, pieces[0].dtype)
    for step, mask in enumerate(masks):
        with jax.named_scope(name):
            arrived = swap(pieces[step], mask)
        out = lax.dynamic_update_slice_in_dim(out, arrived, jnp.bitwise_xor(me, step) * size, axis)
    return out


def after(value, *others):
    return lax.optimization_barrier((value, *others))[0]


def part_of(value, index, count, axis):
    size = value.shape[axis] // count
    return lax.dynamic_slice_in_dim(value, index * size, size, axis)


def sum_spread(name, take, me, masks):
    total = None
    for step, mask in enumerate(masks):
        piece = take(jnp.bitwise_xor(me, step))
        with jax.named_scope(name):
            arrived = swap(piece.astype(BF), mask).astype(F32) if mask else piece.astype(F32)
        total = arrived if total is None else total + arrived
    return total


def sum_spread_f32(name, take, me, masks):
    total = None
    for step, mask in enumerate(masks):
        with jax.named_scope(name):
            arrived = swap(take(jnp.bitwise_xor(me, step)), mask)
        total = arrived if total is None else total + arrived
    return total


def gather(name, value, me, masks, axis):
    return deliver(name, [value] * len(masks), me, masks, axis)


def seq_exchange(name, value):
    with jax.named_scope(name):
        return lax.all_to_all(value, "seq", split_axis=0, concat_axis=0, tiled=True)


def plane_exchange(name, value):
    groups = [list(range(8)), list(range(8, SEQ))]
    with jax.named_scope(name):
        return lax.all_to_all(
            value, "seq", split_axis=0, concat_axis=0, axis_index_groups=groups, tiled=True
        )


def group_exchange(name, value):
    groups = [list(range(first, first + GROUP)) for first in range(0, CHAN, GROUP)]
    with jax.named_scope(name):
        return lax.all_to_all(
            value, "chan", split_axis=0, concat_axis=0, axis_index_groups=groups, tiled=True
        )


def line_exchange(name, value):
    groups = [
        [(z_hi * 8 + plane) * CHAN + block * GROUP + z_lo for z_hi in range(2) for z_lo in range(GROUP)]
        for plane in range(8)
        for block in range(BLOCKS)
    ]
    with jax.named_scope(name):
        return lax.all_to_all(
            value, ("seq", "chan"), split_axis=0, concat_axis=0, axis_index_groups=groups, tiled=True
        )


def lower_mask(size):
    return jnp.arange(size)[:, None] >= jnp.arange(size)[None, :]


def weight_core(terms, core):
    count, rows, width = terms.shape
    split = terms.reshape(count, 8, 2, rows // 16, width)
    pair = sum_spread(
        "weight_core", lambda other: lax.dynamic_index_in_dim(split, other, 2, keepdims=False), core, CORE
    )
    return pair.reshape(count, 2, 4, rows // 16, width)


def weight_line(pair, x):
    return sum_spread(
        "weight_x", lambda other: lax.dynamic_index_in_dim(pair, other, 2, keepdims=False), x, X
    )


def weight_z(line, z_lo):
    return sum_spread("weight_z", lambda other: part_of(line, other, 4, 3), z_lo, Z_LO)


def weight_z_hi(line, z_hi):
    return sum_spread(
        "weight_z_hi", lambda other: lax.dynamic_index_in_dim(line, other, 1, keepdims=False), z_hi, Z_HI
    )


def body(
    layer_input,
    query_scale,
    key_scale,
    twiddle,
    seq_inner,
    seq_outer,
    grad_output,
    hidden_pre,
    up_right,
    up_left,
    down_right,
    down_left,
):
    outer_here, inner_len = twiddle.shape
    tokens, width = layer_input.shape
    outer_len = seq_outer.shape[0]
    hidden = hidden_pre.shape[1]
    quarter = tokens // GROUP
    seq = lax.axis_index("seq")
    chan = lax.axis_index("chan")
    z_lo, y = chan % 4, chan // 4
    core, x, z_hi = seq % 2, (seq // 2) % 4, seq // 8
    mine = width // SEQ
    inner_mask = lower_mask(inner_len)
    outer_mask = lower_mask(outer_len)
    inner_tri = jnp.where(inner_mask, seq_inner, jnp.zeros_like(seq_inner))
    outer_tri = jnp.where(outer_mask, seq_outer, jnp.zeros_like(seq_outer))
    layer_t = layer_input.T
    grad_t = grad_output.T
    piece = quarter // BLOCKS

    right = jnp.stack([down_right[0], up_right[0].T])
    right = part_of(right, core * 4 + x, 8, 1)

    grad_pieces = pieces_for(lambda other: part_of(grad_t, other, 4, 1), z_lo, Z_LO, (right,))
    layer_rows = layer_t.reshape(SEQ, mine * outer_here, inner_len)
    twiddle_high = twiddle.astype(BF)
    twiddle_low = (twiddle - twiddle_high.astype(F32)).astype(BF)
    twiddle_parts = jnp.concatenate([twiddle_high, twiddle_low], axis=0)
    twiddle_parts = jnp.broadcast_to(twiddle_parts, (SEQ,) + twiddle_parts.shape)
    right = gather("right_z", right, z_lo, Z_LO, 2)
    grad_rows = deliver("grad_z", grad_pieces, z_lo, Z_LO, 0)
    pre_send = after(hidden_pre.reshape(GROUP, quarter, hidden), grad_rows, right)
    pre_values = group_exchange("hidden_pre_z", pre_send)
    pre_values = pre_values.transpose(1, 0, 2).reshape(quarter, 4 * hidden)
    pre_values = lax.optimization_barrier(pre_values)
    right = gather("right_x", right, x, X, 1)

    grad_pieces = pieces_for(lambda other: part_of(grad_rows, other, 4, 1), y, Y)
    grad_blocks = deliver("grad_y", [p[None] for p in grad_pieces], y, Y, 0).astype(F32)
    left_down = down_left.astype(F32)
    down_mix = jnp.stack(
        [
            sum(left_down[j, k][:, None] * grad_blocks[j] for j in range(BLOCKS)).astype(BF)
            for k in range(BLOCKS)
        ]
    )
    down_pieces = pieces_for(
        lambda other: lax.dynamic_index_in_dim(down_mix, other, 0, keepdims=False), y, Y, (right,)
    )
    right = gather("right_core", right, core, CORE, 1)
    down_grad = deliver("down_y", down_pieces, y, Y, 1)

    layer_send = after(jnp.concatenate([layer_rows, twiddle_parts], axis=1), pre_values)
    layer_cols = seq_exchange("layer_seq", layer_send)

    def to_cols(value):
        return (
            value.reshape(SEQ, mine, outer_here, inner_len)
            .transpose(1, 0, 2, 3)
            .reshape(mine, outer_len, inner_len)
        )

    def to_rows(value):
        return (
            value.reshape(mine, SEQ, outer_here, inner_len)
            .transpose(1, 0, 2, 3)
            .reshape(SEQ, mine * outer_here, inner_len)
        )

    def blocks_to_cols(value):
        by_line = value.reshape(GROUP, 2, width // 2, quarter).transpose(1, 0, 2, 3)
        by_line = line_exchange("cols_z", by_line.reshape(8, width // 2, quarter))
        by_line = by_line.reshape(2, GROUP, 8, mine, outer_here // GROUP, inner_len)
        by_line = by_line.transpose(2, 3, 0, 1, 4, 5).reshape(8, mine * 2 * outer_here, inner_len)
        by_plane = plane_exchange("cols_plane", by_line)
        by_plane = by_plane.reshape(8, mine, 2, outer_here, inner_len).transpose(1, 2, 0, 3, 4)
        return by_plane.reshape(mine, outer_len, inner_len)

    def mixed_send(value):
        by_plane = value.reshape(mine, 2, 8, outer_here, inner_len).transpose(2, 0, 1, 3, 4)
        by_plane = plane_exchange("blocks_plane", by_plane.reshape(8, mine * 2 * outer_here, inner_len))
        return by_plane

    def mixed_arrive(by_plane):
        by_line = by_plane.reshape(width // 2, 2, outer_here, inner_len).transpose(1, 0, 2, 3)
        by_line = by_line.reshape(2, width // 2, GROUP, quarter).transpose(0, 2, 1, 3)
        by_line = by_line.reshape(8, width // 2, quarter)
        arrived = line_exchange("blocks_z", by_line)
        return arrived.reshape(2, GROUP, width // 2, quarter).transpose(1, 0, 2, 3).reshape(4 * width, quarter)

    layer_cols, twiddle_high, twiddle_low = jnp.split(
        layer_cols, [mine * outer_here, mine * outer_here + outer_here], axis=1
    )
    twiddle_all = (twiddle_high.astype(F32) + twiddle_low.astype(F32)).reshape(outer_len, inner_len)
    layer_cols = to_cols(layer_cols).astype(F32)
    key_mine = part_of(key_scale, seq, SEQ, 0)[:, None, None]
    query_mine = part_of(query_scale, seq, SEQ, 0)[:, None, None]
    key_input = (layer_cols * key_mine).astype(BF)
    first_pass = (
        jnp.einsum("bk,cak->cab", inner_tri, key_input, preferred_element_type=F32) * twiddle_all
    ).astype(BF)
    convolved = jnp.einsum("ij,cjb->cib", outer_tri, first_pass, preferred_element_type=F32).astype(BF)
    mixed = (layer_cols + layer_cols * query_mine * convolved.astype(F32)).astype(BF)
    mixed_plane = mixed_send(mixed)

    hidden_grad = jnp.einsum("pt,pq->tq", down_grad, right[0], preferred_element_type=F32)
    pre_f = pre_values.astype(F32)
    activated = jax.nn.gelu(pre_f).astype(BF)
    pre_grad = jax.vjp(jax.nn.gelu, pre_f)[1](hidden_grad)[0].astype(BF)
    down_terms = jnp.einsum("pt,tq->pq", down_grad, activated, preferred_element_type=F32)
    mix_pieces = pieces_for(lambda other: part_of(pre_grad, other, 4, 0)[None], y, Y)
    pre_blocks = deliver("pre_y", mix_pieces, y, Y, 0)
    pre_blocks = pre_blocks.astype(F32)
    left_up = up_left.astype(F32)
    right_mix = jnp.stack(
        [
            sum(left_up[j, k][None, :] * pre_blocks[j] for j in range(BLOCKS)).astype(BF)
            for k in range(BLOCKS)
        ]
    )
    right_pieces = pieces_for(
        lambda other: lax.dynamic_index_in_dim(right_mix, other, 0, keepdims=False), y, Y
    )
    right_grad = deliver("right_y", right_pieces, y, Y, 0)
    right_grad, mixed_plane = lax.optimization_barrier((right_grad, mixed_plane))
    partial_value = jnp.einsum("pq,tq->pt", right[1], right_grad, preferred_element_type=F32)
    mix_grad = (grad_rows.astype(F32) + partial_value).astype(BF)

    mix_grad = blocks_to_cols(mix_grad)
    mix_grad, mixed_plane = lax.optimization_barrier((mix_grad, mixed_plane))
    mixed_rows = mixed_arrive(mixed_plane)
    up_terms = jnp.einsum("pt,tq->pq", mixed_rows, right_grad, preferred_element_type=F32)
    weight_sums = weight_core(jnp.stack([down_terms, up_terms]), core)
    mix_grad = mix_grad.astype(F32)
    conv_f = convolved.astype(F32)
    grad_layer = mix_grad * layer_cols
    conv_grad = (grad_layer * query_mine).astype(BF)
    query_terms = jnp.sum(grad_layer * conv_f, axis=(1, 2))
    first_grad = jnp.einsum("ij,cib->cjb", outer_tri, conv_grad, preferred_element_type=F32).astype(BF)
    outer_terms = jnp.einsum("cib,cjb->ij", conv_grad, first_pass, preferred_element_type=F32)
    back_pass = (first_grad.astype(F32) * twiddle_all).astype(BF)
    key_grad = jnp.einsum("bk,cab->cak", inner_tri, back_pass, preferred_element_type=F32)
    inner_terms = jnp.einsum("cab,cak->bk", back_pass, key_input, preferred_element_type=F32)
    key_terms = jnp.sum(key_grad * layer_cols, axis=(1, 2))
    grad_input = (mix_grad * (1.0 + query_mine * conv_f) + key_mine * key_grad).astype(BF)
    grad_input = seq_exchange("grad_input_seq", to_rows(grad_input))

    side = 128
    count = inner_len // side
    tiles = [
        inner_terms[i * side : (i + 1) * side, j * side : (j + 1) * side]
        for i in range(count)
        for j in range(i + 1)
    ]
    model = CHAN * width
    at = chan * width + seq * mine
    scales = jnp.zeros((2, model), F32)
    scales = lax.dynamic_update_slice(scales, jnp.stack([query_terms, key_terms]), (0, at))
    scale_rows = 2 * model // side
    sums = jnp.concatenate(tiles + [outer_terms, scales.reshape(scale_rows, side)], axis=0)
    whole_rows = -(-sums.shape[0] // 512) * 512
    sums = jnp.pad(sums, ((0, whole_rows - sums.shape[0]), (0, 0)))
    for me, masks in ((y, Y), (z_lo, Z_LO)):
        sums = sum_spread_f32("sums", lambda other, sums=sums: part_of(sums, other, 4, 0), me, masks)
    sums = sum_spread_f32("sums", lambda other, sums=sums: sums, x, X)
    sums, weight_sums = lax.optimization_barrier((sums, weight_sums))
    weight_sums = weight_line(weight_sums, x)
    sums = sum_spread_f32("sums", lambda other, sums=sums: sums, x, join(Z_HI, CORE))
    sums, weight_sums, grad_input = lax.optimization_barrier((sums, weight_sums, grad_input))
    weight_sums = weight_z(weight_sums, z_lo)
    sums = gather("sums_back", sums, z_lo, Z_LO, 0)
    sums, weight_sums = lax.optimization_barrier((sums, weight_sums))
    weight_sums = weight_z_hi(weight_sums, z_hi)
    sums = gather("sums_back", sums, y, Y, 0)
    blank = jnp.zeros((side, side), F32)
    rows, taken = [], 0
    for i in range(count):
        rows.append(
            jnp.concatenate(
                [sums[(taken + j) * side : (taken + j + 1) * side] for j in range(i + 1)]
                + [blank] * (count - 1 - i),
                axis=1,
            )
        )
        taken += i + 1
    inner_total = jnp.where(inner_mask, jnp.concatenate(rows, axis=0), 0.0)
    outer_total = jnp.where(outer_mask, sums[taken * side : (taken + 1) * side], 0.0)
    scale_total = sums[(taken + 1) * side : (taken + 1) * side + scale_rows].reshape(2, model)
    scale_total = lax.dynamic_slice_in_dim(scale_total, chan * width, width, 1)

    token_scale = (SEQ * tokens) ** (-0.5)
    weights = weight_sums * token_scale
    grad_down, grad_up = weights[0], weights[1].T
    return (
        grad_input.reshape(width, tokens).T,
        grad_up[None],
        grad_down[None],
        scale_total[0] * token_scale,
        scale_total[1] * token_scale,
        inner_total * (outer_len * model) ** (-0.5),
        outer_total * (inner_len * model) ** (-0.5),
    )


def solution(mesh):
    return jax.shard_map(
        body,
        mesh=mesh,
        in_specs=(
            P("seq", "chan"),
            P("chan"),
            P("chan"),
            P("seq", None),
            P(),
            P(),
            P("seq", "chan"),
            P("seq", "chan"),
            P("chan", None, None),
            P(),
            P("chan", None, None),
            P(),
        ),
        out_specs=(
            P("seq", "chan"),
            P("chan", None, "seq"),
            P("chan", "seq", None),
            P("chan"),
            P("chan"),
            P(),
            P(),
        ),
        check_vma=False,
    )
```
